32 devices in a mesh: row: 4 (over y, x), col: 8 (over z, core).
Axes of the slice: x: 2, y: 2, z: 4, core: 2. Of those that a mesh axis runs over, the one named last changes fastest.
Arguments:
- amplitudes: bfloat16 [8192, 1024], P('col', 'row'), may hold values from -6 to 6
- integrals: bfloat16 [1024, 4096], P('col', 'row'), may hold values from -0.5 to 0.5
- sym_mask: int32 [8, 32], replicated, may hold values from 0 to 1, as said below
Outputs:
- ladder: bfloat16 [8192, 4096], P('col', 'row')
The draws below stay inside these ranges and needn't reach their ends.
Inputs may be any that keep to these rules, and one draw needn't show every extreme that they name: sym_mask[k, a] is 1 exactly when cd tile k and ab tile a carry the same one of 8 irreducible representations; among the 8 ab tiles of one index of row, at most 2 carry the same representation.
All inputs are finite; a program needn't handle non-finite values.
Results may differ from the reference program's by a relative error of at most 0.001.
Values may be sent and summed in bfloat16 or wider, within the bound.
A program may use at most 64 MiB of HBM per device.

```python
import jax
import jax.numpy as jnp

TILE = 128
AB_TILES = 8
NIJ = 8192
NCD = 1024
NAB = 4096
N_ROW = 4
N_COL = 8


def draw_sym_mask(key, part):
    table = jnp.array([0, 0, 0, 0, 1, 1, 1, 2, 2, 3, 3, 4, 5, 5, 6, 7], jnp.int32)
    cd_irrep = table[jax.random.randint(jax.random.fold_in(key, 11), (N_COL,), 0, 16)]

    def one_block(index):
        block_key = jax.random.fold_in(jax.random.fold_in(key, 23), index)
        first = cd_irrep[index % N_COL]
        others = (first + 1 + jax.random.permutation(jax.random.fold_in(block_key, 1), 7)[:AB_TILES - 2].astype(jnp.int32)) % 8
        labels = jnp.concatenate([jnp.stack([first, first]), others.astype(jnp.int32)])
        return labels[jax.random.permutation(jax.random.fold_in(block_key, 2), AB_TILES)]
    ab_irrep = jax.vmap(one_block)(jnp.arange(N_ROW, dtype=jnp.int32)).reshape(-1)
    return (cd_irrep[:, None] == ab_irrep[None, :]).astype(jnp.int32)


def steps_of(rng, shape, split, least, largest):
    loudness = 1.0
    for axis_at, blocks in split:
        draws = jax.random.uniform(jax.random.fold_in(jax.random.fold_in(rng, 6), axis_at), (blocks,), jnp.float32, least / len(split), largest / len(split))
        loudness = loudness * jnp.repeat(jnp.exp(draws), shape[axis_at] // blocks).reshape((-1,) + (1,) * (len(shape) - 1 - axis_at))
    return loudness


def scatter_about(stream_key, shape, deviation, limit, pieces=(), held_as=jnp.bfloat16):
    result = jax.random.normal(stream_key, shape, jnp.float32) * deviation
    if len(pieces) > 0:
        result = steps_of(stream_key, shape, pieces, -0.22, 0.18) * result
    return jnp.clip(result, min=-limit, max=limit).astype(held_as)


def setup_inputs(seed: int = 0) -> dict:
    keys = jax.random.split(jax.random.key(seed), 4)
    amplitudes = scatter_about(keys[0], (NIJ, NCD), 1.0, 6.0, ((0, 8), (1, 4)))
    integrals = scatter_about(keys[1], (NCD, NAB), (NCD // 8) ** -0.5, 0.5, ((0, 8), (1, 4)))
    sym_mask = draw_sym_mask(jax.random.fold_in(keys[3], 71), 0)
    return {"amplitudes": amplitudes, "integrals": integrals, "sym_mask": sym_mask}


def reference(amplitudes, integrals, sym_mask):
    expanded = jnp.repeat(jnp.repeat(sym_mask, TILE, axis=0), TILE, axis=1)
    masked = integrals * expanded.astype(jnp.bfloat16)
    return jnp.dot(amplitudes, masked, preferred_element_type=jnp.float32).astype(jnp.bfloat16)
```

```python
import functools

import jax
import jax.numpy as jnp
from jax import lax
from jax.experimental import pallas as pl
from jax.experimental.pallas import tpu as pltpu
from jax.sharding import PartitionSpec as P

TILE = 128
SLOTS = 2
CHUNKS = 8
WINDOW = 2
MESH = pl.DeviceIdType.MESH


def kernel(n_row, n_col, amps, ints, mask, out, rows_all, dense, comp, ints_v, out_v,
           local_sem, out_sem, own_send, fwd_send, amp_recv, v_send, v_recv, s_send):
    ni, nj = 2, n_row // 2
    row, col = lax.axis_index("row"), lax.axis_index("col")
    i, j = row // nj, row % nj
    n_ij, n_cd = amps.shape
    n_ab = ints.shape[1]
    n_tiles = n_ab // TILE
    step_rows = n_ij // CHUNKS

    own_copy = pltpu.make_async_copy(
        amps, rows_all.at[:, pl.ds(pl.multiple_of(row * n_cd, n_cd), n_cd)], local_sem.at[0])
    ints_copy = pltpu.make_async_copy(ints, ints_v, local_sem.at[1])
    ints_copy.start()
    own_copy.start()

    same_i = [i * nj + (j + d) % nj for d in range(1, nj)]
    same_j = [((i + d) % ni) * nj + j for d in range(1, ni)]
    near = same_i + same_j
    peers = [(col + 2 * d) % n_col for d in range(1, n_col // 2)]
    sibling = col + 1 - 2 * (col % 2)

    barrier = pltpu.get_barrier_semaphore()
    for peer in near:
        pl.semaphore_signal(barrier, inc=1, device_id={"row": peer}, device_id_type=MESH)
    for peer in peers + [sibling]:
        pl.semaphore_signal(barrier, inc=1, device_id={"col": peer}, device_id_type=MESH)
    pl.semaphore_wait(barrier, len(near) + len(peers) + 1)

    def part(source, c):
        return rows_all.at[pl.ds(c * step_rows, step_rows),
                           pl.ds(pl.multiple_of(source * n_cd, n_cd), n_cd)]

    def own(c, d):
        return pltpu.make_async_remote_copy(
            src_ref=amps.at[pl.ds(c * step_rows, step_rows)], dst_ref=part(row, c),
            send_sem=own_send.at[d, c], recv_sem=amp_recv.at[row, c],
            device_id={"row": near[d]}, device_id_type=MESH)

    def forwards(c):
        sources, targets = (same_i, same_j) if c % 2 == 0 else (same_j, same_i)
        return [[pltpu.make_async_remote_copy(
            src_ref=part(source, c), dst_ref=part(source, c),
            send_sem=fwd_send.at[a * len(targets) + b, c], recv_sem=amp_recv.at[source, c],
            device_id={"row": target}, device_id_type=MESH)
            for b, target in enumerate(targets)] for a, source in enumerate(sources)]

    def arrive(source, c):
        pltpu.make_async_copy(part(source, c), part(source, c), amp_recv.at[source, c]).wait()

    def start_own(c):
        for d in range(len(near)):
            own(c, d).start()

    for c in range(WINDOW):
        start_own(c)

    def slot_weights(k):
        seen = jnp.int32(0)
        weights = []
        for t in range(n_tiles):
            m = mask[k, row * n_tiles + t]
            weights.append(((m * (1 - jnp.minimum(seen, 1))).astype(jnp.float32),
                            (m * jnp.minimum(seen, 1)).astype(jnp.float32)))
            seen = seen + m
        return weights

    ints_copy.wait()
    weights = slot_weights(col)
    for s in range(SLOTS):
        total = jnp.zeros((TILE, TILE), jnp.float32)
        for t in range(n_tiles):
            total += ints_v[:, t * TILE:(t + 1) * TILE].astype(jnp.float32) * weights[t][s]
        comp[col, s] = total.astype(jnp.bfloat16)

    def v_copy(d):
        return pltpu.make_async_remote_copy(
            src_ref=comp.at[col], dst_ref=comp.at[col], send_sem=v_send.at[d], recv_sem=v_recv.at[col],
            device_id={"col": peers[d]}, device_id_type=MESH)

    def sibling_copy(d):
        source = col if d == 0 else peers[d - 1]
        return pltpu.make_async_remote_copy(
            src_ref=comp.at[source], dst_ref=comp.at[source], send_sem=s_send.at[d],
            recv_sem=v_recv.at[source], device_id={"col": sibling}, device_id_type=MESH)

    def v_arrive(source):
        pltpu.make_async_copy(comp.at[source], comp.at[source], v_recv.at[source]).wait()

    for d in range(len(peers)):
        v_copy(d).start()
    sibling_copy(0).start()

    def build_dense():
        def one(k, carry):
            first = comp[k, 0].astype(jnp.float32)
            second = comp[k, 1].astype(jnp.float32)
            w = slot_weights(k)
            for t in range(n_tiles):
                dense[pl.ds(pl.multiple_of(k * TILE, TILE), TILE), t * TILE:(t + 1) * TILE] = (
                    first * w[t][0] + second * w[t][1]).astype(jnp.bfloat16)
            return carry
        lax.fori_loop(0, n_col, one, 0)

    def out_copy(c):
        span = pl.ds(c * step_rows, step_rows)
        return pltpu.make_async_copy(out_v.at[span], out.at[span], out_sem.at[c])

    def multiply(c):
        corner = [(i2, j2) for i2 in range(1, ni) for j2 in range(1, nj)]
        for di, dj in corner:
            arrive(((i + di) % ni) * nj + (j + dj) % nj, c)
        span = slice(c * step_rows, (c + 1) * step_rows)
        width = 2 * TILE
        for at in range(0, n_ab, width):
            out_v[span, at:at + width] = jnp.dot(
                rows_all[span, :], dense[:, at:at + width],
                preferred_element_type=jnp.float32).astype(jnp.bfloat16)
        out_copy(c).start()

    def take(c):
        copies = forwards(c)
        sources, others = (same_i, same_j) if c % 2 == 0 else (same_j, same_i)
        for source, group in zip(sources, copies):
            arrive(source, c)
            for copy in group:
                copy.start()
        for source in others:
            arrive(source, c)

    lag = 3
    for c in range(CHUNKS):
        if c + WINDOW < CHUNKS:
            start_own(c + WINDOW)
        take(c)
        if c == 2:
            for d in range(len(peers)):
                v_arrive(peers[d])
                sibling_copy(d + 1).start()
        if c == 3:
            own_copy.wait()
            v_arrive(sibling)
            for d in range(len(peers)):
                v_arrive((sibling + 2 * (d + 1)) % n_col)
            build_dense()
        if c >= 4:
            multiply(c - 4)
    for c in range(CHUNKS - 4, CHUNKS):
        multiply(c)

    for c in range(CHUNKS):
        for d in range(len(near)):
            own(c, d).wait_send()
        for group in forwards(c):
            for copy in group:
                copy.wait_send()
    for d in range(len(peers)):
        v_copy(d).wait_send()
    for d in range(len(peers) + 1):
        sibling_copy(d).wait_send()
    for c in range(CHUNKS):
        out_copy(c).wait()


def shards(n_row, n_col, amplitudes, integrals, sym_mask):
    n_ij, n_cd = amplitudes.shape
    n_ab = integrals.shape[1]
    near = 1 + n_row // 2 - 1
    dma = pltpu.SemaphoreType.DMA
    return pl.pallas_call(
        functools.partial(kernel, n_row, n_col),
        out_shape=jax.ShapeDtypeStruct((n_ij, n_ab), jnp.bfloat16),
        in_specs=[pl.BlockSpec(memory_space=pl.ANY), pl.BlockSpec(memory_space=pl.ANY),
                  pl.BlockSpec(memory_space=pltpu.SMEM)],
        out_specs=pl.BlockSpec(memory_space=pl.ANY),
        scratch_shapes=[
            pltpu.VMEM((n_ij, n_cd * n_row), jnp.bfloat16),
            pltpu.VMEM((n_col * TILE, n_ab), jnp.bfloat16),
            pltpu.VMEM((n_col, SLOTS, TILE, TILE), jnp.bfloat16),
            pltpu.VMEM((TILE, n_ab), jnp.bfloat16),
            pltpu.VMEM((n_ij, n_ab), jnp.bfloat16),
            dma((2,)),
            dma((CHUNKS,)),
            dma((near, CHUNKS)),
            dma((max(n_row // 2 - 1, 1), CHUNKS)),
            dma((n_row, CHUNKS)),
            dma((n_col // 2,)),
            dma((n_col,)),
            dma((n_col // 2,)),
        ],
        cost_estimate=pl.CostEstimate(
            flops=2 * n_ij * n_ab * n_cd * n_row, bytes_accessed=6 * n_ij * n_ab, transcendentals=0),
        compiler_params=pltpu.CompilerParams(
            collective_id=0, has_side_effects=True, vmem_limit_bytes=48 * 1024 * 1024),
    )(amplitudes, integrals, sym_mask)


def solution(mesh):
    placed = (P("col", "row"), P("col", "row"), P())
    return jax.shard_map(
        functools.partial(shards, mesh.shape["row"], mesh.shape["col"]),
        mesh=mesh, in_specs=placed, out_specs=P("col", "row"), check_vma=False,
    )
```

```python
import functools

import jax
import jax.numpy as jnp
from jax import lax
from jax.experimental import pallas as pl
from jax.experimental.pallas import tpu as pltpu
from jax.sharding import PartitionSpec as P

TILE = 128
SLOTS = 2
CHUNKS = 8
WINDOW = 4
MESH = pl.DeviceIdType.MESH


def kernel(n_row, n_col, amps, ints, mask_hbm, out, rows_all, dense, comp, ints_v, out_v, mask,
           ready_z, ready_core, local_sem, out_sem, own_send, fwd_send, amp_recv, v_send, v_recv, s_send):
    ni, nj = 2, n_row // 2
    row, col = lax.axis_index("row"), lax.axis_index("col")
    i, j = row // nj, row % nj
    n_ij, n_cd = amps.shape
    n_ab = ints.shape[1]
    n_tiles = n_ab // TILE
    step_rows = n_ij // CHUNKS

    own_copy = pltpu.make_async_copy(
        amps, rows_all.at[:, pl.ds(pl.multiple_of(row * n_cd, n_cd), n_cd)], local_sem.at[0])
    ints_copy = pltpu.make_async_copy(ints, ints_v, local_sem.at[1])
    mask_copy = pltpu.make_async_copy(mask_hbm, mask, local_sem.at[2])

    same_i = [i * nj + (j + d) % nj for d in range(1, nj)]
    same_j = [((i + d) % ni) * nj + j for d in range(1, ni)]
    near = same_i + same_j
    n_z = n_col // 2
    z, core = col // 2, col % 2
    peers = [(z + d) % n_z for d in range(1, n_z)]
    sibling = col + 1 - 2 * core

    barrier = pltpu.get_barrier_semaphore()
    for peer in near:
        pl.semaphore_signal(barrier, inc=1, device_id={"row": peer}, device_id_type=MESH)
    for peer in peers:
        @pl.when(peer > z)
        def _():
            pl.semaphore_signal(
                barrier, inc=1, device_id={"col": 2 * peer + core}, device_id_type=MESH)

    @pl.when(core == 0)
    def _():
        pl.semaphore_signal(barrier, inc=1, device_id={"col": sibling}, device_id_type=MESH)

    ints_copy.start()
    mask_copy.start()
    own_copy.start()
    pl.semaphore_wait(barrier, len(near) + z + core)

    def part(source, c):
        return rows_all.at[pl.ds(c * step_rows, step_rows),
                           pl.ds(pl.multiple_of(source * n_cd, n_cd), n_cd)]

    def own(c, d):
        return pltpu.make_async_remote_copy(
            src_ref=amps.at[pl.ds(c * step_rows, step_rows)], dst_ref=part(row, c),
            send_sem=own_send.at[d, c], recv_sem=amp_recv.at[row, c],
            device_id={"row": near[d]}, device_id_type=MESH)

    def forwards(c):
        sources, targets = (same_i, same_j) if c % 2 == 0 else (same_j, same_i)
        return [[pltpu.make_async_remote_copy(
            src_ref=part(source, c), dst_ref=part(source, c),
            send_sem=fwd_send.at[a * len(targets) + b, c], recv_sem=amp_recv.at[source, c],
            device_id={"row": target}, device_id_type=MESH)
            for b, target in enumerate(targets)] for a, source in enumerate(sources)]

    def arrive(source, c):
        pltpu.make_async_copy(part(source, c), part(source, c), amp_recv.at[source, c]).wait()

    def start_own(c):
        for d in range(len(near)):
            own(c, d).start()

    for c in range(WINDOW):
        start_own(c)

    def slot_weights(k):
        seen = jnp.int32(0)
        weights = []
        for t in range(n_tiles):
            m = mask[k, row * n_tiles + t]
            weights.append(((m * (1 - jnp.minimum(seen, 1))).astype(jnp.float32),
                            (m * jnp.minimum(seen, 1)).astype(jnp.float32)))
            seen = seen + m
        return weights

    for peer in peers:
        @pl.when(peer < z)
        def _():
            pl.semaphore_signal(
                ready_z.at[z], inc=1, device_id={"col": 2 * peer + core}, device_id_type=MESH)

    @pl.when(core == 1)
    def _():
        pl.semaphore_signal(ready_core, inc=1, device_id={"col": sibling}, device_id_type=MESH)

    ints_copy.wait()
    mask_copy.wait()
    weights = slot_weights(col)
    for s in range(SLOTS):
        total = jnp.zeros((TILE, TILE), jnp.float32)
        for t in range(n_tiles):
            total += ints_v[:, t * TILE:(t + 1) * TILE].astype(jnp.float32) * weights[t][s]
        comp[col, s] = total.astype(jnp.bfloat16)

    def v_copy(d):
        return pltpu.make_async_remote_copy(
            src_ref=comp.at[col], dst_ref=comp.at[col], send_sem=v_send.at[d], recv_sem=v_recv.at[col],
            device_id={"col": 2 * peers[d] + core}, device_id_type=MESH)

    def sibling_copy(d):
        source = col if d == 0 else 2 * peers[d - 1] + core
        return pltpu.make_async_remote_copy(
            src_ref=comp.at[source], dst_ref=comp.at[source], send_sem=s_send.at[d],
            recv_sem=v_recv.at[source], device_id={"col": sibling}, device_id_type=MESH)

    def v_arrive(source):
        pltpu.make_async_copy(comp.at[source], comp.at[source], v_recv.at[source]).wait()


    def build_dense():
        def one(k, carry):
            first = comp[k, 0].astype(jnp.float32)
            second = comp[k, 1].astype(jnp.float32)
            w = slot_weights(k)
            for t in range(n_tiles):
                dense[pl.ds(pl.multiple_of(k * TILE, TILE), TILE), t * TILE:(t + 1) * TILE] = (
                    first * w[t][0] + second * w[t][1]).astype(jnp.bfloat16)
            return carry
        lax.fori_loop(0, n_col, one, 0)

    def out_copy(c):
        span = pl.ds(c * step_rows, step_rows)
        return pltpu.make_async_copy(out_v.at[span], out.at[span], out_sem.at[c])

    def multiply(c):
        corner = [(i2, j2) for i2 in range(1, ni) for j2 in range(1, nj)]
        for di, dj in corner:
            arrive(((i + di) % ni) * nj + (j + dj) % nj, c)
        span = slice(c * step_rows, (c + 1) * step_rows)
        width = 2 * TILE
        for at in range(0, n_ab, width):
            out_v[span, at:at + width] = jnp.dot(
                rows_all[span, :], dense[:, at:at + width],
                preferred_element_type=jnp.float32).astype(jnp.bfloat16)
        out_copy(c).start()

    def take(c):
        copies = forwards(c)
        sources, others = (same_i, same_j) if c % 2 == 0 else (same_j, same_i)
        for source, group in zip(sources, copies):
            arrive(source, c)
            for copy in group:
                copy.start()
        for source in others:
            arrive(source, c)

    for c in range(CHUNKS):
        if c + WINDOW < CHUNKS:
            start_own(c + WINDOW)
        take(c)
        if c == 0:
            for d, peer in enumerate(peers):
                @pl.when(peer > z)
                def _():
                    pl.semaphore_wait(ready_z.at[peer], 1)
                v_copy(d).start()

            @pl.when(core == 0)
            def _():
                pl.semaphore_wait(ready_core, 1)
            sibling_copy(0).start()
        if c == 3:
            for d, peer in enumerate(peers):
                v_arrive(2 * peer + core)
                sibling_copy(d + 1).start()
        if c == 5:
            own_copy.wait()
            v_arrive(sibling)
            for peer in peers:
                v_arrive(2 * peer + 1 - core)
            build_dense()
            multiply(0)
        if c == 6:
            multiply(1)
            multiply(2)
        if c == 7:
            multiply(3)
    for c in range(4, CHUNKS):
        multiply(c)

    for c in range(CHUNKS):
        for d in range(len(near)):
            own(c, d).wait_send()
        for group in forwards(c):
            for copy in group:
                copy.wait_send()
    for d in range(len(peers)):
        v_copy(d).wait_send()
    for d in range(len(peers) + 1):
        sibling_copy(d).wait_send()
    for c in range(CHUNKS):
        out_copy(c).wait()


def shards(n_row, n_col, amplitudes, integrals, sym_mask):
    n_ij, n_cd = amplitudes.shape
    n_ab = integrals.shape[1]
    near = 1 + n_row // 2 - 1
    dma = pltpu.SemaphoreType.DMA
    return pl.pallas_call(
        functools.partial(kernel, n_row, n_col),
        out_shape=jax.ShapeDtypeStruct((n_ij, n_ab), jnp.bfloat16),
        in_specs=[pl.BlockSpec(memory_space=pltpu.HBM)] * 3,
        out_specs=pl.BlockSpec(memory_space=pl.ANY),
        scratch_shapes=[
            pltpu.VMEM((n_ij, n_cd * n_row), jnp.bfloat16),
            pltpu.VMEM((n_col * TILE, n_ab), jnp.bfloat16),
            pltpu.VMEM((n_col, SLOTS, TILE, TILE), jnp.bfloat16),
            pltpu.VMEM((TILE, n_ab), jnp.bfloat16),
            pltpu.VMEM((n_ij, n_ab), jnp.bfloat16),
            pltpu.SMEM(sym_mask.shape, jnp.int32),
            pltpu.SemaphoreType.REGULAR((n_col // 2,)),
            pltpu.SemaphoreType.REGULAR,
            dma((3,)),
            dma((CHUNKS,)),
            dma((near, CHUNKS)),
            dma((max(n_row // 2 - 1, 1), CHUNKS)),
            dma((n_row, CHUNKS)),
            dma((n_col // 2,)),
            dma((n_col,)),
            dma((n_col // 2,)),
        ],
        cost_estimate=pl.CostEstimate(
            flops=2 * n_ij * n_ab * n_cd * n_row, bytes_accessed=6 * n_ij * n_ab, transcendentals=0),
        compiler_params=pltpu.CompilerParams(
            collective_id=0, has_side_effects=True, vmem_limit_bytes=48 * 1024 * 1024),
    )(*(pltpu.with_memory_space_constraint(x, pltpu.HBM) for x in (amplitudes, integrals, sym_mask)))


def solution(mesh):
    placed = (P("col", "row"), P("col", "row"), P())
    return jax.shard_map(
        functools.partial(shards, mesh.shape["row"], mesh.shape["col"]),
        mesh=mesh, in_specs=placed, out_specs=P("col", "row"), check_vma=False,
    )
```

```python
import functools

import jax
import jax.numpy as jnp
from jax import lax
from jax.experimental import pallas as pl
from jax.experimental.pallas import tpu as pltpu
from jax.sharding import PartitionSpec as P

TILE = 128
SLOTS = 2
CHUNKS = 16
WINDOW = 5
GROUPS = ((0, 4, 10), (4, 8, 13), (8, 12, 15), (12, 14, 15), (14, 16, 15))
MESH = pl.DeviceIdType.MESH


def kernel(n_row, n_col, amps, ints, mask_hbm, out, rows_all, dense, comp, ints_v, out_v, mask,
           ready_z, ready_core, local_sem, out_sem, own_send, fwd_send, amp_recv, v_send, v_recv, s_send):
    ni, nj = 2, n_row // 2
    row, col = lax.axis_index("row"), lax.axis_index("col")
    i, j = row // nj, row % nj
    n_ij, n_cd = amps.shape
    n_ab = ints.shape[1]
    n_tiles = n_ab // TILE
    step_rows = n_ij // CHUNKS

    own_copy = pltpu.make_async_copy(
        amps, rows_all.at[:, pl.ds(pl.multiple_of(row * n_cd, n_cd), n_cd)], local_sem.at[0])
    ints_copy = pltpu.make_async_copy(ints, ints_v, local_sem.at[1])
    mask_copy = pltpu.make_async_copy(mask_hbm, mask, local_sem.at[2])

    same_i = [i * nj + (j + d) % nj for d in range(1, nj)]
    same_j = [((i + d) % ni) * nj + j for d in range(1, ni)]
    near = same_i + same_j
    n_z = n_col // 2
    z, core = col // 2, col % 2
    peers = [(z + d) % n_z for d in range(1, n_z)]
    sibling = col + 1 - 2 * core

    barrier = pltpu.get_barrier_semaphore()
    for peer in near:
        pl.semaphore_signal(barrier, inc=1, device_id={"row": peer}, device_id_type=MESH)
    for peer in peers:
        @pl.when(peer > z)
        def _():
            pl.semaphore_signal(
                barrier, inc=1, device_id={"col": 2 * peer + core}, device_id_type=MESH)

    @pl.when(core == 0)
    def _():
        pl.semaphore_signal(barrier, inc=1, device_id={"col": sibling}, device_id_type=MESH)

    ints_copy.start()
    mask_copy.start()
    own_copy.start()
    pl.semaphore_wait(barrier, len(near) + z + core)

    def part(source, c):
        return rows_all.at[pl.ds(c * step_rows, step_rows),
                           pl.ds(pl.multiple_of(source * n_cd, n_cd), n_cd)]

    def own(c, d):
        return pltpu.make_async_remote_copy(
            src_ref=amps.at[pl.ds(c * step_rows, step_rows)], dst_ref=part(row, c),
            send_sem=own_send.at[d, c], recv_sem=amp_recv.at[row, c],
            device_id={"row": near[d]}, device_id_type=MESH)

    def forwards(c):
        sources, targets = (same_i, same_j) if c % 2 == 0 else (same_j, same_i)
        return [[pltpu.make_async_remote_copy(
            src_ref=part(source, c), dst_ref=part(source, c),
            send_sem=fwd_send.at[a * len(targets) + b, c], recv_sem=amp_recv.at[source, c],
            device_id={"row": target}, device_id_type=MESH)
            for b, target in enumerate(targets)] for a, source in enumerate(sources)]

    def arrive(source, c):
        pltpu.make_async_copy(part(source, c), part(source, c), amp_recv.at[source, c]).wait()

    def start_own(c):
        for d in range(len(near)):
            own(c, d).start()

    for c in range(WINDOW):
        start_own(c)

    def slot_weights(k):
        seen = jnp.int32(0)
        weights = []
        for t in range(n_tiles):
            m = mask[k, row * n_tiles + t]
            weights.append(((m * (1 - jnp.minimum(seen, 1))).astype(jnp.float32),
                            (m * jnp.minimum(seen, 1)).astype(jnp.float32)))
            seen = seen + m
        return weights

    for peer in peers:
        @pl.when(peer < z)
        def _():
            pl.semaphore_signal(
                ready_z.at[z], inc=1, device_id={"col": 2 * peer + core}, device_id_type=MESH)

    @pl.when(core == 1)
    def _():
        pl.semaphore_signal(ready_core, inc=1, device_id={"col": sibling}, device_id_type=MESH)

    ints_copy.wait()
    mask_copy.wait()
    weights = slot_weights(col)
    for s in range(SLOTS):
        total = jnp.zeros((TILE, TILE), jnp.float32)
        for t in range(n_tiles):
            total += ints_v[:, t * TILE:(t + 1) * TILE].astype(jnp.float32) * weights[t][s]
        comp[col, s] = total.astype(jnp.bfloat16)

    def v_copy(d):
        return pltpu.make_async_remote_copy(
            src_ref=comp.at[col], dst_ref=comp.at[col], send_sem=v_send.at[d], recv_sem=v_recv.at[col],
            device_id={"col": 2 * peers[d] + core}, device_id_type=MESH)

    def sibling_copy(d):
        source = col if d == 0 else 2 * peers[d - 1] + core
        return pltpu.make_async_remote_copy(
            src_ref=comp.at[source], dst_ref=comp.at[source], send_sem=s_send.at[d],
            recv_sem=v_recv.at[source], device_id={"col": sibling}, device_id_type=MESH)

    def v_arrive(source):
        pltpu.make_async_copy(comp.at[source], comp.at[source], v_recv.at[source]).wait()


    def build_dense(parity):
        def one(u, carry):
            k = 2 * u + parity
            first, second = comp[k, 0], comp[k, 1]
            w = slot_weights(k)
            for t in range(n_tiles):
                dense[pl.ds(pl.multiple_of(k * TILE, TILE), TILE), t * TILE:(t + 1) * TILE] = (
                    first * w[t][0].astype(jnp.bfloat16) + second * w[t][1].astype(jnp.bfloat16))
            return carry
        lax.fori_loop(0, n_z, one, 0)

    def out_copy(g):
        span = pl.ds(GROUPS[g][0] * step_rows, (GROUPS[g][1] - GROUPS[g][0]) * step_rows)
        return pltpu.make_async_copy(out_v.at[span], out.at[span], out_sem.at[g])

    def multiply(g):
        begin, end, _ = GROUPS[g]
        for c in range(begin, end):
            for di in range(1, ni):
                for dj in range(1, nj):
                    arrive(((i + di) % ni) * nj + (j + dj) % nj, c)
        span = slice(begin * step_rows, end * step_rows)
        width = 2 * TILE
        for at in range(0, n_ab, width):
            out_v[span, at:at + width] = jnp.dot(
                rows_all[span, :], dense[:, at:at + width],
                preferred_element_type=jnp.float32).astype(jnp.bfloat16)
        out_copy(g).start()

    def take(c):
        copies = forwards(c)
        sources, others = (same_i, same_j) if c % 2 == 0 else (same_j, same_i)
        for source, group in zip(sources, copies):
            arrive(source, c)
            for copy in group:
                copy.start()
        for source in others:
            arrive(source, c)

    for c in range(CHUNKS):
        if c + WINDOW < CHUNKS:
            start_own(c + WINDOW)
        take(c)
        if c == 0:
            for d, peer in enumerate(peers):
                @pl.when(peer > z)
                def _():
                    pl.semaphore_wait(ready_z.at[peer], 1)
                v_copy(d).start()

            @pl.when(core == 0)
            def _():
                pl.semaphore_wait(ready_core, 1)
            sibling_copy(0).start()
        if c == 5:
            for d, peer in enumerate(peers):
                v_arrive(2 * peer + core)
                sibling_copy(d + 1).start()
        if c == 7:
            build_dense(core)
        if c == 8:
            own_copy.wait()
            v_arrive(sibling)
            for peer in peers:
                v_arrive(2 * peer + 1 - core)
            build_dense(1 - core)
        for g, group in enumerate(GROUPS):
            if group[2] == c:
                multiply(g)

    for c in range(CHUNKS):
        for d in range(len(near)):
            own(c, d).wait_send()
        for group in forwards(c):
            for copy in group:
                copy.wait_send()
    for d in range(len(peers)):
        v_copy(d).wait_send()
    for d in range(len(peers) + 1):
        sibling_copy(d).wait_send()
    for g in range(len(GROUPS)):
        out_copy(g).wait()


def shards(n_row, n_col, amplitudes, integrals, sym_mask):
    n_ij, n_cd = amplitudes.shape
    n_ab = integrals.shape[1]
    near = 1 + n_row // 2 - 1
    dma = pltpu.SemaphoreType.DMA
    return pl.pallas_call(
        functools.partial(kernel, n_row, n_col),
        out_shape=jax.ShapeDtypeStruct((n_ij, n_ab), jnp.bfloat16),
        in_specs=[pl.BlockSpec(memory_space=pltpu.HBM)] * 3,
        out_specs=pl.BlockSpec(memory_space=pl.ANY),
        scratch_shapes=[
            pltpu.VMEM((n_ij, n_cd * n_row), jnp.bfloat16),
            pltpu.VMEM((n_col * TILE, n_ab), jnp.bfloat16),
            pltpu.VMEM((n_col, SLOTS, TILE, TILE), jnp.bfloat16),
            pltpu.VMEM((TILE, n_ab), jnp.bfloat16),
            pltpu.VMEM((n_ij, n_ab), jnp.bfloat16),
            pltpu.SMEM(sym_mask.shape, jnp.int32),
            pltpu.SemaphoreType.REGULAR((n_col // 2,)),
            pltpu.SemaphoreType.REGULAR,
            dma((3,)),
            dma((len(GROUPS),)),
            dma((near, CHUNKS)),
            dma((max(n_row // 2 - 1, 1), CHUNKS)),
            dma((n_row, CHUNKS)),
            dma((n_col // 2,)),
            dma((n_col,)),
            dma((n_col // 2,)),
        ],
        cost_estimate=pl.CostEstimate(
            flops=2 * n_ij * n_ab * n_cd * n_row, bytes_accessed=6 * n_ij * n_ab, transcendentals=0),
        compiler_params=pltpu.CompilerParams(
            collective_id=0, has_side_effects=True, vmem_limit_bytes=48 * 1024 * 1024),
    )(*(pltpu.with_memory_space_constraint(x, pltpu.HBM) for x in (amplitudes, integrals, sym_mask)))


def solution(mesh):
    placed = (P("col", "row"), P("col", "row"), P())
    return jax.shard_map(
        functools.partial(shards, mesh.shape["row"], mesh.shape["col"]),
        mesh=mesh, in_specs=placed, out_specs=P("col", "row"), check_vma=False,
    )
```

```python
import functools

import jax
import jax.numpy as jnp
from jax import lax
from jax.experimental import pallas as pl
from jax.experimental.pallas import tpu as pltpu
from jax.sharding import PartitionSpec as P

TILE = 128
SLOTS = 2
CHUNKS = 8
WINDOW = 8
GROUPS = ((0, 2, 7), (2, 4, 7), (4, 6, 7), (6, 7, 7), (7, 8, 7))
MESH = pl.DeviceIdType.MESH


def kernel(n_row, n_col, amps, ints, mask_hbm, out, rows_all, dense, comp, ints_v, out_v, mask,
           ready_z, ready_core, local_sem, out_sem, own_send, fwd_send, amp_recv, v_send, v_recv, s_send):
    ni, nj = 2, n_row // 2
    row, col = lax.axis_index("row"), lax.axis_index("col")
    i, j = row // nj, row % nj
    n_ij, n_cd = amps.shape
    n_ab = ints.shape[1]
    n_tiles = n_ab // TILE
    step_rows = n_ij // CHUNKS

    own_copy = pltpu.make_async_copy(
        amps, rows_all.at[:, pl.ds(pl.multiple_of(row * n_cd, n_cd), n_cd)], local_sem.at[0])
    ints_copy = pltpu.make_async_copy(ints, ints_v, local_sem.at[1])
    mask_copy = pltpu.make_async_copy(mask_hbm, mask, local_sem.at[2])

    same_i = [i * nj + (j + d) % nj for d in range(1, nj)]
    same_j = [((i + d) % ni) * nj + j for d in range(1, ni)]
    near = same_i + same_j
    n_z = n_col // 2
    z, core = col // 2, col % 2
    peers = [(z + d) % n_z for d in range(1, n_z)]
    sibling = col + 1 - 2 * core

    barrier = pltpu.get_barrier_semaphore()
    for peer in near:
        pl.semaphore_signal(barrier, inc=1, device_id={"row": peer}, device_id_type=MESH)
    for peer in peers:
        @pl.when(peer > z)
        def _():
            pl.semaphore_signal(
                barrier, inc=1, device_id={"col": 2 * peer + core}, device_id_type=MESH)

    @pl.when(core == 0)
    def _():
        pl.semaphore_signal(barrier, inc=1, device_id={"col": sibling}, device_id_type=MESH)

    ints_copy.start()
    mask_copy.start()
    own_copy.start()
    pl.semaphore_wait(barrier, len(near) + z + core)

    def part(source, c):
        return rows_all.at[pl.ds(c * step_rows, step_rows),
                           pl.ds(pl.multiple_of(source * n_cd, n_cd), n_cd)]

    def own(c, d):
        return pltpu.make_async_remote_copy(
            src_ref=amps.at[pl.ds(c * step_rows, step_rows)], dst_ref=part(row, c),
            send_sem=own_send.at[d, c], recv_sem=amp_recv.at[row, c],
            device_id={"row": near[d]}, device_id_type=MESH)

    def forwards(c):
        sources, targets = (same_i, same_j) if c % 2 == 0 else (same_j, same_i)
        return [[pltpu.make_async_remote_copy(
            src_ref=part(source, c), dst_ref=part(source, c),
            send_sem=fwd_send.at[a * len(targets) + b, c], recv_sem=amp_recv.at[source, c],
            device_id={"row": target}, device_id_type=MESH)
            for b, target in enumerate(targets)] for a, source in enumerate(sources)]

    def arrive(source, c):
        pltpu.make_async_copy(part(source, c), part(source, c), amp_recv.at[source, c]).wait()

    def start_own(c):
        for d in range(len(near)):
            own(c, d).start()

    for c in range(WINDOW):
        start_own(c)

    def slot_weights(k):
        seen = jnp.int32(0)
        weights = []
        for t in range(n_tiles):
            m = mask[k, row * n_tiles + t]
            weights.append(((m * (1 - jnp.minimum(seen, 1))).astype(jnp.float32),
                            (m * jnp.minimum(seen, 1)).astype(jnp.float32)))
            seen = seen + m
        return weights

    for peer in peers:
        @pl.when(peer < z)
        def _():
            pl.semaphore_signal(
                ready_z.at[z], inc=1, device_id={"col": 2 * peer + core}, device_id_type=MESH)

    @pl.when(core == 1)
    def _():
        pl.semaphore_signal(ready_core, inc=1, device_id={"col": sibling}, device_id_type=MESH)

    ints_copy.wait()
    mask_copy.wait()
    weights = slot_weights(col)
    for s in range(SLOTS):
        total = jnp.zeros((TILE, TILE), jnp.float32)
        for t in range(n_tiles):
            total += ints_v[:, t * TILE:(t + 1) * TILE].astype(jnp.float32) * weights[t][s]
        comp[col, s] = total.astype(jnp.bfloat16)

    def v_copy(d):
        return pltpu.make_async_remote_copy(
            src_ref=comp.at[col], dst_ref=comp.at[col], send_sem=v_send.at[d], recv_sem=v_recv.at[col],
            device_id={"col": 2 * peers[d] + core}, device_id_type=MESH)

    def sibling_copy(d):
        source = col if d == 0 else 2 * peers[d - 1] + core
        return pltpu.make_async_remote_copy(
            src_ref=comp.at[source], dst_ref=comp.at[source], send_sem=s_send.at[d],
            recv_sem=v_recv.at[source], device_id={"col": sibling}, device_id_type=MESH)

    def v_arrive(source):
        pltpu.make_async_copy(comp.at[source], comp.at[source], v_recv.at[source]).wait()


    def build_dense(parity):
        def one(u, carry):
            k = 2 * u + parity
            first, second = comp[k, 0], comp[k, 1]
            w = slot_weights(k)
            for t in range(n_tiles):
                dense[pl.ds(pl.multiple_of(k * TILE, TILE), TILE), t * TILE:(t + 1) * TILE] = (
                    first * w[t][0].astype(jnp.bfloat16) + second * w[t][1].astype(jnp.bfloat16))
            return carry
        lax.fori_loop(0, n_z, one, 0)

    def out_copy(g):
        span = pl.ds(GROUPS[g][0] * step_rows, (GROUPS[g][1] - GROUPS[g][0]) * step_rows)
        return pltpu.make_async_copy(out_v.at[span], out.at[span], out_sem.at[g])

    def multiply(g):
        begin, end, _ = GROUPS[g]
        for c in range(begin, end):
            for di in range(1, ni):
                for dj in range(1, nj):
                    arrive(((i + di) % ni) * nj + (j + dj) % nj, c)
        span = slice(begin * step_rows, end * step_rows)
        width = 2 * TILE
        for at in range(0, n_ab, width):
            out_v[span, at:at + width] = jnp.dot(
                rows_all[span, :], dense[:, at:at + width],
                preferred_element_type=jnp.float32).astype(jnp.bfloat16)
        out_copy(g).start()

    def take(c):
        copies = forwards(c)
        sources, others = (same_i, same_j) if c % 2 == 0 else (same_j, same_i)
        for source, group in zip(sources, copies):
            arrive(source, c)
            for copy in group:
                copy.start()
        for source in others:
            arrive(source, c)

    for c in range(CHUNKS):
        if c + WINDOW < CHUNKS:
            start_own(c + WINDOW)
        take(c)
        if c == 0:
            for d, peer in enumerate(peers):
                @pl.when(peer > z)
                def _():
                    pl.semaphore_wait(ready_z.at[peer], 1)
                v_copy(d).start()

            @pl.when(core == 0)
            def _():
                pl.semaphore_wait(ready_core, 1)
            sibling_copy(0).start()
        if c == 3:
            for d, peer in enumerate(peers):
                v_arrive(2 * peer + core)
                sibling_copy(d + 1).start()
        if c == 4:
            build_dense(core)
        if c == 5:
            own_copy.wait()
            v_arrive(sibling)
            for peer in peers:
                v_arrive(2 * peer + 1 - core)
            build_dense(1 - core)
        for g, group in enumerate(GROUPS):
            if group[2] == c:
                multiply(g)

    for c in range(CHUNKS):
        for d in range(len(near)):
            own(c, d).wait_send()
        for group in forwards(c):
            for copy in group:
                copy.wait_send()
    for d in range(len(peers)):
        v_copy(d).wait_send()
    for d in range(len(peers) + 1):
        sibling_copy(d).wait_send()
    for g in range(len(GROUPS)):
        out_copy(g).wait()


def shards(n_row, n_col, amplitudes, integrals, sym_mask):
    n_ij, n_cd = amplitudes.shape
    n_ab = integrals.shape[1]
    near = 1 + n_row // 2 - 1
    dma = pltpu.SemaphoreType.DMA
    return pl.pallas_call(
        functools.partial(kernel, n_row, n_col),
        out_shape=jax.ShapeDtypeStruct((n_ij, n_ab), jnp.bfloat16),
        in_specs=[pl.BlockSpec(memory_space=pltpu.HBM)] * 3,
        out_specs=pl.BlockSpec(memory_space=pl.ANY),
        scratch_shapes=[
            pltpu.VMEM((n_ij, n_cd * n_row), jnp.bfloat16),
            pltpu.VMEM((n_col * TILE, n_ab), jnp.bfloat16),
            pltpu.VMEM((n_col, SLOTS, TILE, TILE), jnp.bfloat16),
            pltpu.VMEM((TILE, n_ab), jnp.bfloat16),
            pltpu.VMEM((n_ij, n_ab), jnp.bfloat16),
            pltpu.SMEM(sym_mask.shape, jnp.int32),
            pltpu.SemaphoreType.REGULAR((n_col // 2,)),
            pltpu.SemaphoreType.REGULAR,
            dma((3,)),
            dma((len(GROUPS),)),
            dma((near, CHUNKS)),
            dma((max(n_row // 2 - 1, 1), CHUNKS)),
            dma((n_row, CHUNKS)),
            dma((n_col // 2,)),
            dma((n_col,)),
            dma((n_col // 2,)),
        ],
        cost_estimate=pl.CostEstimate(
            flops=2 * n_ij * n_ab * n_cd * n_row, bytes_accessed=6 * n_ij * n_ab, transcendentals=0),
        compiler_params=pltpu.CompilerParams(
            collective_id=0, has_side_effects=True, vmem_limit_bytes=48 * 1024 * 1024),
    )(*(pltpu.with_memory_space_constraint(x, pltpu.HBM) for x in (amplitudes, integrals, sym_mask)))


def solution(mesh):
    placed = (P("col", "row"), P("col", "row"), P())
    return jax.shard_map(
        functools.partial(shards, mesh.shape["row"], mesh.shape["col"]),
        mesh=mesh, in_specs=placed, out_specs=P("col", "row"), check_vma=False,
    )
```

```python
import functools

import jax
import jax.numpy as jnp
from jax import lax
from jax.experimental import pallas as pl
from jax.experimental.pallas import tpu as pltpu
from jax.sharding import PartitionSpec as P

TILE = 128
SLOTS = 2
CHUNKS = 8
WINDOW = 8
GROUPS = ((0, 2, 7), (2, 4, 7), (4, 6, 7), (6, 7, 7), (7, 8, 7))
MESH = pl.DeviceIdType.MESH


def kernel(n_row, n_col, amps, ints, mask_hbm, out, rows_all, dense, comp, ints_v, mask,
           ready_z, ready_core, local_sem, own_send, fwd_send, amp_recv, v_send, v_recv, s_send):
    ni, nj = 2, n_row // 2
    row, col = lax.axis_index("row"), lax.axis_index("col")
    i, j = row // nj, row % nj
    n_ij, n_cd = amps.shape
    n_ab = ints.shape[1]
    n_tiles = n_ab // TILE
    step_rows = n_ij // CHUNKS

    own_copy = pltpu.make_async_copy(
        amps, rows_all.at[:, pl.ds(pl.multiple_of(row * n_cd, n_cd), n_cd)], local_sem.at[0])
    ints_copy = pltpu.make_async_copy(ints, ints_v, local_sem.at[1])
    mask_copy = pltpu.make_async_copy(mask_hbm, mask, local_sem.at[2])

    same_i = [i * nj + (j + d) % nj for d in range(1, nj)]
    same_j = [((i + d) % ni) * nj + j for d in range(1, ni)]
    near = same_i + same_j
    n_z = n_col // 2
    z, core = col // 2, col % 2
    peers = [(z + d) % n_z for d in range(1, n_z)]
    sibling = col + 1 - 2 * core

    barrier = pltpu.get_barrier_semaphore()
    for peer in near:
        pl.semaphore_signal(barrier, inc=1, device_id={"row": peer}, device_id_type=MESH)
    for peer in peers:
        @pl.when(peer > z)
        def _():
            pl.semaphore_signal(
                barrier, inc=1, device_id={"col": 2 * peer + core}, device_id_type=MESH)

    @pl.when(core == 0)
    def _():
        pl.semaphore_signal(barrier, inc=1, device_id={"col": sibling}, device_id_type=MESH)

    ints_copy.start()
    mask_copy.start()
    own_copy.start()
    pl.semaphore_wait(barrier, len(near) + z + core)

    def part(source, c):
        return rows_all.at[pl.ds(c * step_rows, step_rows),
                           pl.ds(pl.multiple_of(source * n_cd, n_cd), n_cd)]

    def own(c, d):
        return pltpu.make_async_remote_copy(
            src_ref=amps.at[pl.ds(c * step_rows, step_rows)], dst_ref=part(row, c),
            send_sem=own_send.at[d, c], recv_sem=amp_recv.at[row, c],
            device_id={"row": near[d]}, device_id_type=MESH)

    def forwards(c):
        sources, targets = (same_i, same_j) if c % 2 == 0 else (same_j, same_i)
        return [[pltpu.make_async_remote_copy(
            src_ref=part(source, c), dst_ref=part(source, c),
            send_sem=fwd_send.at[a * len(targets) + b, c], recv_sem=amp_recv.at[source, c],
            device_id={"row": target}, device_id_type=MESH)
            for b, target in enumerate(targets)] for a, source in enumerate(sources)]

    def arrive(source, c):
        pltpu.make_async_copy(part(source, c), part(source, c), amp_recv.at[source, c]).wait()

    def start_own(c):
        for d in range(len(near)):
            own(c, d).start()

    for c in range(WINDOW):
        start_own(c)

    def slot_weights(k):
        seen = jnp.int32(0)
        weights = []
        for t in range(n_tiles):
            m = mask[k, row * n_tiles + t]
            weights.append(((m * (1 - jnp.minimum(seen, 1))).astype(jnp.float32),
                            (m * jnp.minimum(seen, 1)).astype(jnp.float32)))
            seen = seen + m
        return weights

    for peer in peers:
        @pl.when(peer < z)
        def _():
            pl.semaphore_signal(
                ready_z.at[z], inc=1, device_id={"col": 2 * peer + core}, device_id_type=MESH)

    @pl.when(core == 1)
    def _():
        pl.semaphore_signal(ready_core, inc=1, device_id={"col": sibling}, device_id_type=MESH)

    ints_copy.wait()
    mask_copy.wait()
    weights = slot_weights(col)
    for s in range(SLOTS):
        total = jnp.zeros((TILE, TILE), jnp.float32)
        for t in range(n_tiles):
            total += ints_v[:, t * TILE:(t + 1) * TILE].astype(jnp.float32) * weights[t][s]
        comp[col, s] = total.astype(jnp.bfloat16)

    def v_copy(d):
        return pltpu.make_async_remote_copy(
            src_ref=comp.at[col], dst_ref=comp.at[col], send_sem=v_send.at[d], recv_sem=v_recv.at[col],
            device_id={"col": 2 * peers[d] + core}, device_id_type=MESH)

    def sibling_copy(d):
        source = col if d == 0 else 2 * peers[d - 1] + core
        return pltpu.make_async_remote_copy(
            src_ref=comp.at[source], dst_ref=comp.at[source], send_sem=s_send.at[d],
            recv_sem=v_recv.at[source], device_id={"col": sibling}, device_id_type=MESH)

    def v_arrive(source):
        pltpu.make_async_copy(comp.at[source], comp.at[source], v_recv.at[source]).wait()


    def build_dense(parity):
        def one(u, carry):
            k = 2 * u + parity
            first, second = comp[k, 0], comp[k, 1]
            w = slot_weights(k)
            for t in range(n_tiles):
                dense[pl.ds(pl.multiple_of(k * TILE, TILE), TILE), t * TILE:(t + 1) * TILE] = (
                    first * w[t][0].astype(jnp.bfloat16) + second * w[t][1].astype(jnp.bfloat16))
            return carry
        lax.fori_loop(0, n_z, one, 0)

    def multiply(g):
        begin, end, _ = GROUPS[g]
        for c in range(begin, end):
            for di in range(1, ni):
                for dj in range(1, nj):
                    arrive(((i + di) % ni) * nj + (j + dj) % nj, c)
        span = slice(begin * step_rows, end * step_rows)
        width = 2 * TILE
        for at in range(0, n_ab, width):
            out[span, at:at + width] = jnp.dot(
                rows_all[span, :], dense[:, at:at + width],
                preferred_element_type=jnp.float32).astype(jnp.bfloat16)

    def take(c):
        copies = forwards(c)
        sources, others = (same_i, same_j) if c % 2 == 0 else (same_j, same_i)
        for source, group in zip(sources, copies):
            arrive(source, c)
            for copy in group:
                copy.start()
        for source in others:
            arrive(source, c)

    for c in range(CHUNKS):
        if c + WINDOW < CHUNKS:
            start_own(c + WINDOW)
        take(c)
        if c == 0:
            for d, peer in enumerate(peers):
                @pl.when(peer > z)
                def _():
                    pl.semaphore_wait(ready_z.at[peer], 1)
                v_copy(d).start()

            @pl.when(core == 0)
            def _():
                pl.semaphore_wait(ready_core, 1)
            sibling_copy(0).start()
        if c == 3:
            for d, peer in enumerate(peers):
                v_arrive(2 * peer + core)
                sibling_copy(d + 1).start()
        if c == 4:
            build_dense(core)
        if c == 5:
            own_copy.wait()
            v_arrive(sibling)
            for peer in peers:
                v_arrive(2 * peer + 1 - core)
            build_dense(1 - core)
        for g, group in enumerate(GROUPS):
            if group[2] == c:
                multiply(g)

    for c in range(CHUNKS):
        for d in range(len(near)):
            own(c, d).wait_send()
        for group in forwards(c):
            for copy in group:
                copy.wait_send()
    for d in range(len(peers)):
        v_copy(d).wait_send()
    for d in range(len(peers) + 1):
        sibling_copy(d).wait_send()


def shards(n_row, n_col, amplitudes, integrals, sym_mask):
    n_ij, n_cd = amplitudes.shape
    n_ab = integrals.shape[1]
    near = 1 + n_row // 2 - 1
    dma = pltpu.SemaphoreType.DMA
    return pl.pallas_call(
        functools.partial(kernel, n_row, n_col),
        out_shape=jax.ShapeDtypeStruct((n_ij, n_ab), jnp.bfloat16),
        in_specs=[pl.BlockSpec(memory_space=pltpu.HBM)] * 3,
        out_specs=pl.BlockSpec(memory_space=pltpu.VMEM),
        scratch_shapes=[
            pltpu.VMEM((n_ij, n_cd * n_row), jnp.bfloat16),
            pltpu.VMEM((n_col * TILE, n_ab), jnp.bfloat16),
            pltpu.VMEM((n_col, SLOTS, TILE, TILE), jnp.bfloat16),
            pltpu.VMEM((TILE, n_ab), jnp.bfloat16),
            pltpu.SMEM(sym_mask.shape, jnp.int32),
            pltpu.SemaphoreType.REGULAR((n_col // 2,)),
            pltpu.SemaphoreType.REGULAR,
            dma((3,)),
            dma((near, CHUNKS)),
            dma((max(n_row // 2 - 1, 1), CHUNKS)),
            dma((n_row, CHUNKS)),
            dma((n_col // 2,)),
            dma((n_col,)),
            dma((n_col // 2,)),
        ],
        cost_estimate=pl.CostEstimate(
            flops=2 * n_ij * n_ab * n_cd * n_row, bytes_accessed=6 * n_ij * n_ab, transcendentals=0),
        compiler_params=pltpu.CompilerParams(
            collective_id=0, has_side_effects=True, vmem_limit_bytes=48 * 1024 * 1024),
    )(*(pltpu.with_memory_space_constraint(x, pltpu.HBM) for x in (amplitudes, integrals, sym_mask)))


def solution(mesh):
    placed = (P("col", "row"), P("col", "row"), P())
    return jax.shard_map(
        functools.partial(shards, mesh.shape["row"], mesh.shape["col"]),
        mesh=mesh, in_specs=placed, out_specs=P("col", "row"), check_vma=False,
    )
```

```python
import functools

import jax
import jax.numpy as jnp
from jax import lax
from jax.experimental import pallas as pl
from jax.experimental.pallas import tpu as pltpu
from jax.sharding import PartitionSpec as P

TILE = 128
SLOTS = 2
CHUNKS = 8
WINDOW = 8
GROUPS = ((0, 2), (2, 4), (4, 6))
LAST = (6, 8)
MESH = pl.DeviceIdType.MESH


def kernel(n_row, n_col, amps, ints, mask_hbm, out, rows_all, dense, comp, ints_v, partial, mask,
           ready_z, ready_core, local_sem, own_send, fwd_send, amp_recv, v_send, v_recv, s_send):
    ni, nj = 2, n_row // 2
    row, col = lax.axis_index("row"), lax.axis_index("col")
    i, j = row // nj, row % nj
    n_ij, n_cd = amps.shape
    n_ab = ints.shape[1]
    n_tiles = n_ab // TILE
    step_rows = n_ij // CHUNKS

    own_copy = pltpu.make_async_copy(
        amps, rows_all.at[:, pl.ds(pl.multiple_of(row * n_cd, n_cd), n_cd)], local_sem.at[0])
    ints_copy = pltpu.make_async_copy(ints, ints_v, local_sem.at[1])
    mask_copy = pltpu.make_async_copy(mask_hbm, mask, local_sem.at[2])

    same_i = [i * nj + (j + d) % nj for d in range(1, nj)]
    same_j = [((i + d) % ni) * nj + j for d in range(1, ni)]
    near = same_i + same_j
    n_z = n_col // 2
    z, core = col // 2, col % 2
    peers = [(z + d) % n_z for d in range(1, n_z)]
    sibling = col + 1 - 2 * core

    barrier = pltpu.get_barrier_semaphore()
    for peer in near:
        pl.semaphore_signal(barrier, inc=1, device_id={"row": peer}, device_id_type=MESH)
    for peer in peers:
        @pl.when(peer > z)
        def _():
            pl.semaphore_signal(
                barrier, inc=1, device_id={"col": 2 * peer + core}, device_id_type=MESH)

    @pl.when(core == 0)
    def _():
        pl.semaphore_signal(barrier, inc=1, device_id={"col": sibling}, device_id_type=MESH)

    ints_copy.start()
    mask_copy.start()
    own_copy.start()
    pl.semaphore_wait(barrier, len(near) + z + core)

    def part(source, c):
        return rows_all.at[pl.ds(c * step_rows, step_rows),
                           pl.ds(pl.multiple_of(source * n_cd, n_cd), n_cd)]

    def own(c, d):
        return pltpu.make_async_remote_copy(
            src_ref=amps.at[pl.ds(c * step_rows, step_rows)], dst_ref=part(row, c),
            send_sem=own_send.at[d, c], recv_sem=amp_recv.at[row, c],
            device_id={"row": near[d]}, device_id_type=MESH)

    def forwards(c):
        sources, targets = (same_i, same_j) if c % 2 == 0 else (same_j, same_i)
        return [[pltpu.make_async_remote_copy(
            src_ref=part(source, c), dst_ref=part(source, c),
            send_sem=fwd_send.at[a * len(targets) + b, c], recv_sem=amp_recv.at[source, c],
            device_id={"row": target}, device_id_type=MESH)
            for b, target in enumerate(targets)] for a, source in enumerate(sources)]

    def arrive(source, c):
        pltpu.make_async_copy(part(source, c), part(source, c), amp_recv.at[source, c]).wait()

    def start_own(c):
        for d in range(len(near)):
            own(c, d).start()

    for c in range(WINDOW):
        start_own(c)

    def slot_weights(k):
        seen = jnp.int32(0)
        weights = []
        for t in range(n_tiles):
            m = mask[k, row * n_tiles + t]
            weights.append(((m * (1 - jnp.minimum(seen, 1))).astype(jnp.float32),
                            (m * jnp.minimum(seen, 1)).astype(jnp.float32)))
            seen = seen + m
        return weights

    for peer in peers:
        @pl.when(peer < z)
        def _():
            pl.semaphore_signal(
                ready_z.at[z], inc=1, device_id={"col": 2 * peer + core}, device_id_type=MESH)

    @pl.when(core == 1)
    def _():
        pl.semaphore_signal(ready_core, inc=1, device_id={"col": sibling}, device_id_type=MESH)

    ints_copy.wait()
    mask_copy.wait()
    weights = slot_weights(col)
    for s in range(SLOTS):
        total = jnp.zeros((TILE, TILE), jnp.float32)
        for t in range(n_tiles):
            total += ints_v[:, t * TILE:(t + 1) * TILE].astype(jnp.float32) * weights[t][s]
        comp[col, s] = total.astype(jnp.bfloat16)

    def v_copy(d):
        return pltpu.make_async_remote_copy(
            src_ref=comp.at[col], dst_ref=comp.at[col], send_sem=v_send.at[d], recv_sem=v_recv.at[col],
            device_id={"col": 2 * peers[d] + core}, device_id_type=MESH)

    def sibling_copy(d):
        source = col if d == 0 else 2 * peers[d - 1] + core
        return pltpu.make_async_remote_copy(
            src_ref=comp.at[source], dst_ref=comp.at[source], send_sem=s_send.at[d],
            recv_sem=v_recv.at[source], device_id={"col": sibling}, device_id_type=MESH)

    def v_arrive(source):
        pltpu.make_async_copy(comp.at[source], comp.at[source], v_recv.at[source]).wait()


    def build_dense(parity):
        def one(u, carry):
            k = 2 * u + parity
            first, second = comp[k, 0], comp[k, 1]
            w = slot_weights(k)
            for t in range(n_tiles):
                dense[pl.ds(pl.multiple_of(k * TILE, TILE), TILE), t * TILE:(t + 1) * TILE] = (
                    first * w[t][0].astype(jnp.bfloat16) + second * w[t][1].astype(jnp.bfloat16))
            return carry
        lax.fori_loop(0, n_z, one, 0)

    corner = [((i + di) % ni) * nj + (j + dj) % nj for di in range(1, ni) for dj in range(1, nj)]
    width = 2 * TILE

    def arrive_corner(begin, end):
        for c in range(begin, end):
            for source in corner:
                arrive(source, c)

    def multiply(begin, end):
        arrive_corner(begin, end)
        span = slice(begin * step_rows, end * step_rows)
        for at in range(0, n_ab, width):
            out[span, at:at + width] = jnp.dot(
                rows_all[span, :], dense[:, at:at + width],
                preferred_element_type=jnp.float32).astype(jnp.bfloat16)

    last = slice(LAST[0] * step_rows, LAST[1] * step_rows)

    def last_dot(sources, at):
        total = None
        for source in sources:
            depth = pl.ds(pl.multiple_of(source * n_cd, n_cd), n_cd)
            product = jnp.dot(rows_all[last, depth], dense[depth, at:at + width],
                              preferred_element_type=jnp.float32)
            total = product if total is None else total + product
        return total

    def take(c):
        copies = forwards(c)
        sources, others = (same_i, same_j) if c % 2 == 0 else (same_j, same_i)
        for source, group in zip(sources, copies):
            arrive(source, c)
            for copy in group:
                copy.start()
        for source in others:
            arrive(source, c)

    for c in range(CHUNKS):
        if c + WINDOW < CHUNKS:
            start_own(c + WINDOW)
        take(c)
        if c == 0:
            for d, peer in enumerate(peers):
                @pl.when(peer > z)
                def _():
                    pl.semaphore_wait(ready_z.at[peer], 1)
                v_copy(d).start()

            @pl.when(core == 0)
            def _():
                pl.semaphore_wait(ready_core, 1)
            sibling_copy(0).start()
        if c == 3:
            for d, peer in enumerate(peers):
                v_arrive(2 * peer + core)
                sibling_copy(d + 1).start()
        if c == 4:
            build_dense(core)
        if c == 5:
            own_copy.wait()
            v_arrive(sibling)
            for peer in peers:
                v_arrive(2 * peer + 1 - core)
            build_dense(1 - core)

    for begin, end in GROUPS[:-1]:
        multiply(begin, end)
    for at in range(0, n_ab, width):
        partial[:, at:at + width] = last_dot([row] + near, at)
    multiply(*GROUPS[-1])
    arrive_corner(*LAST)
    for at in range(0, n_ab, width):
        out[last, at:at + width] = (
            partial[:, at:at + width] + last_dot(corner, at)).astype(jnp.bfloat16)

    for c in range(CHUNKS):
        for d in range(len(near)):
            own(c, d).wait_send()
        for group in forwards(c):
            for copy in group:
                copy.wait_send()
    for d in range(len(peers)):
        v_copy(d).wait_send()
    for d in range(len(peers) + 1):
        sibling_copy(d).wait_send()


def shards(n_row, n_col, amplitudes, integrals, sym_mask):
    n_ij, n_cd = amplitudes.shape
    n_ab = integrals.shape[1]
    near = 1 + n_row // 2 - 1
    dma = pltpu.SemaphoreType.DMA
    return pl.pallas_call(
        functools.partial(kernel, n_row, n_col),
        out_shape=jax.ShapeDtypeStruct((n_ij, n_ab), jnp.bfloat16),
        in_specs=[pl.BlockSpec(memory_space=pltpu.HBM)] * 3,
        out_specs=pl.BlockSpec(memory_space=pltpu.VMEM),
        scratch_shapes=[
            pltpu.VMEM((n_ij, n_cd * n_row), jnp.bfloat16),
            pltpu.VMEM((n_col * TILE, n_ab), jnp.bfloat16),
            pltpu.VMEM((n_col, SLOTS, TILE, TILE), jnp.bfloat16),
            pltpu.VMEM((TILE, n_ab), jnp.bfloat16),
            pltpu.VMEM(((LAST[1] - LAST[0]) * n_ij // CHUNKS, n_ab), jnp.float32),
            pltpu.SMEM(sym_mask.shape, jnp.int32),
            pltpu.SemaphoreType.REGULAR((n_col // 2,)),
            pltpu.SemaphoreType.REGULAR,
            dma((3,)),
            dma((near, CHUNKS)),
            dma((max(n_row // 2 - 1, 1), CHUNKS)),
            dma((n_row, CHUNKS)),
            dma((n_col // 2,)),
            dma((n_col,)),
            dma((n_col // 2,)),
        ],
        cost_estimate=pl.CostEstimate(
            flops=2 * n_ij * n_ab * n_cd * n_row, bytes_accessed=6 * n_ij * n_ab, transcendentals=0),
        compiler_params=pltpu.CompilerParams(
            collective_id=0, has_side_effects=True, vmem_limit_bytes=48 * 1024 * 1024),
    )(*(pltpu.with_memory_space_constraint(x, pltpu.HBM) for x in (amplitudes, integrals, sym_mask)))


def solution(mesh):
    placed = (P("col", "row"), P("col", "row"), P())
    return jax.shard_map(
        functools.partial(shards, mesh.shape["row"], mesh.shape["col"]),
        mesh=mesh, in_specs=placed, out_specs=P("col", "row"), check_vma=False,
    )
```

```python
import functools

import jax
import jax.numpy as jnp
from jax import lax
from jax.experimental import pallas as pl
from jax.experimental.pallas import tpu as pltpu
from jax.sharding import PartitionSpec as P

TILE = 128
SLOTS = 2
CHUNKS = 4
WINDOW = 4
GROUPS = ((0, 1), (1, 2), (2, 3))
LAST = (3, 4)
MESH = pl.DeviceIdType.MESH


def kernel(n_row, n_col, amps, ints, mask_hbm, out, rows_all, dense, comp, ints_v, partial, mask,
           ready_z, ready_core, local_sem, own_send, fwd_send, amp_recv, v_send, v_recv, s_send):
    ni, nj = 2, n_row // 2
    row, col = lax.axis_index("row"), lax.axis_index("col")
    i, j = row // nj, row % nj
    n_ij, n_cd = amps.shape
    n_ab = ints.shape[1]
    n_tiles = n_ab // TILE
    step_rows = n_ij // CHUNKS

    own_copy = pltpu.make_async_copy(
        amps, rows_all.at[:, pl.ds(pl.multiple_of(row * n_cd, n_cd), n_cd)], local_sem.at[0])
    ints_copy = pltpu.make_async_copy(ints, ints_v, local_sem.at[1])
    mask_copy = pltpu.make_async_copy(mask_hbm, mask, local_sem.at[2])

    same_i = [i * nj + (j + d) % nj for d in range(1, nj)]
    same_j = [((i + d) % ni) * nj + j for d in range(1, ni)]
    near = same_i + same_j
    n_z = n_col // 2
    z, core = col // 2, col % 2
    peers = [(z + d) % n_z for d in range(1, n_z)]
    sibling = col + 1 - 2 * core

    barrier = pltpu.get_barrier_semaphore()
    for peer in near:
        pl.semaphore_signal(barrier, inc=1, device_id={"row": peer}, device_id_type=MESH)
    for peer in peers:
        @pl.when(peer > z)
        def _():
            pl.semaphore_signal(
                barrier, inc=1, device_id={"col": 2 * peer + core}, device_id_type=MESH)

    @pl.when(core == 0)
    def _():
        pl.semaphore_signal(barrier, inc=1, device_id={"col": sibling}, device_id_type=MESH)

    ints_copy.start()
    mask_copy.start()
    own_copy.start()
    pl.semaphore_wait(barrier, len(near) + z + core)

    def part(source, c):
        return rows_all.at[pl.ds(c * step_rows, step_rows),
                           pl.ds(pl.multiple_of(source * n_cd, n_cd), n_cd)]

    def own(c, d):
        return pltpu.make_async_remote_copy(
            src_ref=amps.at[pl.ds(c * step_rows, step_rows)], dst_ref=part(row, c),
            send_sem=own_send.at[d, c], recv_sem=amp_recv.at[row, c],
            device_id={"row": near[d]}, device_id_type=MESH)

    def forwards(c):
        sources, targets = (same_i, same_j) if c % 2 == 0 else (same_j, same_i)
        return [[pltpu.make_async_remote_copy(
            src_ref=part(source, c), dst_ref=part(source, c),
            send_sem=fwd_send.at[a * len(targets) + b, c], recv_sem=amp_recv.at[source, c],
            device_id={"row": target}, device_id_type=MESH)
            for b, target in enumerate(targets)] for a, source in enumerate(sources)]

    def arrive(source, c):
        pltpu.make_async_copy(part(source, c), part(source, c), amp_recv.at[source, c]).wait()

    def start_own(c):
        for d in range(len(near)):
            own(c, d).start()

    for c in range(WINDOW):
        start_own(c)

    def slot_weights(k):
        seen = jnp.int32(0)
        weights = []
        for t in range(n_tiles):
            m = mask[k, row * n_tiles + t]
            weights.append(((m * (1 - jnp.minimum(seen, 1))).astype(jnp.float32),
                            (m * jnp.minimum(seen, 1)).astype(jnp.float32)))
            seen = seen + m
        return weights

    for peer in peers:
        @pl.when(peer < z)
        def _():
            pl.semaphore_signal(
                ready_z.at[z], inc=1, device_id={"col": 2 * peer + core}, device_id_type=MESH)

    @pl.when(core == 1)
    def _():
        pl.semaphore_signal(ready_core, inc=1, device_id={"col": sibling}, device_id_type=MESH)

    ints_copy.wait()
    mask_copy.wait()
    weights = slot_weights(col)
    for s in range(SLOTS):
        total = jnp.zeros((TILE, TILE), jnp.float32)
        for t in range(n_tiles):
            total += ints_v[:, t * TILE:(t + 1) * TILE].astype(jnp.float32) * weights[t][s]
        comp[col, s] = total.astype(jnp.bfloat16)

    def v_copy(d):
        return pltpu.make_async_remote_copy(
            src_ref=comp.at[col], dst_ref=comp.at[col], send_sem=v_send.at[d], recv_sem=v_recv.at[col],
            device_id={"col": 2 * peers[d] + core}, device_id_type=MESH)

    def sibling_copy(d):
        source = col if d == 0 else 2 * peers[d - 1] + core
        return pltpu.make_async_remote_copy(
            src_ref=comp.at[source], dst_ref=comp.at[source], send_sem=s_send.at[d],
            recv_sem=v_recv.at[source], device_id={"col": sibling}, device_id_type=MESH)

    def v_arrive(source):
        pltpu.make_async_copy(comp.at[source], comp.at[source], v_recv.at[source]).wait()


    def build_dense(parity):
        def one(u, carry):
            k = 2 * u + parity
            first, second = comp[k, 0], comp[k, 1]
            w = slot_weights(k)
            for t in range(n_tiles):
                dense[pl.ds(pl.multiple_of(k * TILE, TILE), TILE), t * TILE:(t + 1) * TILE] = (
                    first * w[t][0].astype(jnp.bfloat16) + second * w[t][1].astype(jnp.bfloat16))
            return carry
        lax.fori_loop(0, n_z, one, 0)

    corner = [((i + di) % ni) * nj + (j + dj) % nj for di in range(1, ni) for dj in range(1, nj)]
    width = 2 * TILE

    def arrive_corner(begin, end):
        for c in range(begin, end):
            for source in corner:
                arrive(source, c)

    def multiply(begin, end):
        arrive_corner(begin, end)
        span = slice(begin * step_rows, end * step_rows)
        for at in range(0, n_ab, width):
            out[span, at:at + width] = jnp.dot(
                rows_all[span, :], dense[:, at:at + width],
                preferred_element_type=jnp.float32).astype(jnp.bfloat16)

    last = slice(LAST[0] * step_rows, LAST[1] * step_rows)

    def last_dot(sources, at):
        total = None
        for source in sources:
            depth = pl.ds(pl.multiple_of(source * n_cd, n_cd), n_cd)
            product = jnp.dot(rows_all[last, depth], dense[depth, at:at + width],
                              preferred_element_type=jnp.float32)
            total = product if total is None else total + product
        return total

    def take(c):
        copies = forwards(c)
        sources, others = (same_i, same_j) if c % 2 == 0 else (same_j, same_i)
        for source, group in zip(sources, copies):
            arrive(source, c)
            for copy in group:
                copy.start()
        for source in others:
            arrive(source, c)

    for c in range(CHUNKS):
        if c + WINDOW < CHUNKS:
            start_own(c + WINDOW)
        take(c)
        if c == 0:
            for d, peer in enumerate(peers):
                @pl.when(peer > z)
                def _():
                    pl.semaphore_wait(ready_z.at[peer], 1)
                v_copy(d).start()

            @pl.when(core == 0)
            def _():
                pl.semaphore_wait(ready_core, 1)
            sibling_copy(0).start()
        if c == 1:
            for d, peer in enumerate(peers):
                v_arrive(2 * peer + core)
                sibling_copy(d + 1).start()
        if c == 1:
            build_dense(core)
        if c == 2:
            own_copy.wait()
            v_arrive(sibling)
            for peer in peers:
                v_arrive(2 * peer + 1 - core)
            build_dense(1 - core)

    for begin, end in GROUPS[:-1]:
        multiply(begin, end)
    for at in range(0, n_ab, width):
        partial[:, at:at + width] = last_dot([row] + near, at)
    multiply(*GROUPS[-1])
    arrive_corner(*LAST)
    for at in range(0, n_ab, width):
        out[last, at:at + width] = (
            partial[:, at:at + width] + last_dot(corner, at)).astype(jnp.bfloat16)

    for c in range(CHUNKS):
        for d in range(len(near)):
            own(c, d).wait_send()
        for group in forwards(c):
            for copy in group:
                copy.wait_send()
    for d in range(len(peers)):
        v_copy(d).wait_send()
    for d in range(len(peers) + 1):
        sibling_copy(d).wait_send()


def shards(n_row, n_col, amplitudes, integrals, sym_mask):
    n_ij, n_cd = amplitudes.shape
    n_ab = integrals.shape[1]
    near = 1 + n_row // 2 - 1
    dma = pltpu.SemaphoreType.DMA
    return pl.pallas_call(
        functools.partial(kernel, n_row, n_col),
        out_shape=jax.ShapeDtypeStruct((n_ij, n_ab), jnp.bfloat16),
        in_specs=[pl.BlockSpec(memory_space=pltpu.HBM)] * 3,
        out_specs=pl.BlockSpec(memory_space=pltpu.VMEM),
        scratch_shapes=[
            pltpu.VMEM((n_ij, n_cd * n_row), jnp.bfloat16),
            pltpu.VMEM((n_col * TILE, n_ab), jnp.bfloat16),
            pltpu.VMEM((n_col, SLOTS, TILE, TILE), jnp.bfloat16),
            pltpu.VMEM((TILE, n_ab), jnp.bfloat16),
            pltpu.VMEM(((LAST[1] - LAST[0]) * n_ij // CHUNKS, n_ab), jnp.float32),
            pltpu.SMEM(sym_mask.shape, jnp.int32),
            pltpu.SemaphoreType.REGULAR((n_col // 2,)),
            pltpu.SemaphoreType.REGULAR,
            dma((3,)),
            dma((near, CHUNKS)),
            dma((max(n_row // 2 - 1, 1), CHUNKS)),
            dma((n_row, CHUNKS)),
            dma((n_col // 2,)),
            dma((n_col,)),
            dma((n_col // 2,)),
        ],
        cost_estimate=pl.CostEstimate(
            flops=2 * n_ij * n_ab * n_cd * n_row, bytes_accessed=6 * n_ij * n_ab, transcendentals=0),
        compiler_params=pltpu.CompilerParams(
            collective_id=0, has_side_effects=True, vmem_limit_bytes=48 * 1024 * 1024),
    )(*(pltpu.with_memory_space_constraint(x, pltpu.HBM) for x in (amplitudes, integrals, sym_mask)))


def solution(mesh):
    placed = (P("col", "row"), P("col", "row"), P())
    return jax.shard_map(
        functools.partial(shards, mesh.shape["row"], mesh.shape["col"]),
        mesh=mesh, in_specs=placed, out_specs=P("col", "row"), check_vma=False,
    )
```
